512 devices in a mesh: rep: 128 (over z, y, x_lo), tp: 4 (over x_hi, core).
Axes of the slice: x: 4 (x_hi: 2, x_lo: 2; x = x_hi * 2 + x_lo), y: 8, z: 8, core: 2. Of those that a mesh axis runs over, the one named last changes fastest.
Arguments:
- tokens: bfloat16 [16384, 2560], P('rep', 'tp'), may hold values from -6 to 6
- weights: bfloat16 [128, 2560, 1728], P('rep', 'tp'), may hold values from -6 to 6
- push_scale: bfloat16 [128, 4], P('rep', 'tp'), may hold values from 0.5 to 2
- cotangent: bfloat16 [128, 1728, 512], P('rep', 'tp'), may hold values from -6 to 6
- step_count: int32 [1], replicated, may hold values from 0 to 999
Outputs:
- mixed_weights: bfloat16 [128, 2560, 1728], P('rep', 'tp')
- mixed_scale: float32 [128, 4], P('rep', 'tp')
The draws below stay inside these ranges and needn't reach their ends.
All inputs are finite; a program needn't handle non-finite values.
Results may differ from the reference program's by a relative error of at most 0.006.
Values may be sent and summed in bfloat16 or wider, within the bound.
A program may use at most 128 MiB of HBM per device.

```python
import math
import jax
import jax.numpy as jnp
from jax import lax

D = 2560
QUARTER_FF = 1728
TOK_GROUP = 512
REPLICAS = 32
TOKENS = 16384
N_REP = 128
N_TP = 4


def steps_of(stream_key, shape, shards, low, top_value):
    level = 1.0
    for position, blocks in shards:
        draws = jax.random.uniform(jax.random.fold_in(jax.random.fold_in(stream_key, 6), position), (blocks,), jnp.float32, low / len(shards), top_value / len(shards))
        level = level * jnp.repeat(jnp.exp(draws), shape[position] // blocks).reshape((-1,) + (1,) * (len(shape) - 1 - position))
    return level


def gaussian(rng, dims, scale, reach, pieces=(), held_as=jnp.bfloat16):
    array = jax.random.normal(rng, dims, jnp.float32) * scale
    if len(pieces) > 0:
        array = steps_of(rng, dims, pieces, -0.22, 0.18) * array
    return jnp.clip(array, min=-reach, max=reach).astype(held_as)


def setup_inputs(seed: int = 0) -> dict:
    arg_keys = jax.random.split(jax.random.key(seed), 6)
    tokens = gaussian(arg_keys[0], (TOKENS, D), 1.0, 6.0, ((0, 128), (1, 4)))
    weights = gaussian(arg_keys[1], (N_REP, D, QUARTER_FF), 1.0, 6.0, ((0, 128), (1, 4)))
    push_scale = jnp.clip(jnp.exp(math.log(2.0) - 1.3862944 * jax.random.uniform(arg_keys[2], (N_REP, N_TP), jnp.float32) ** steps_of(arg_keys[2], (N_REP, N_TP), ((0, 128), (1, 4)), -0.2, 0.2)), 0.5, 2.0).astype(jnp.bfloat16)
    cotangent = gaussian(arg_keys[3], (N_REP, QUARTER_FF, TOK_GROUP), 1.0, 6.0, ((0, 128), (1, 4)))
    step_count = jax.random.randint(arg_keys[4], (1,), 0, 1000).astype(jnp.int32)
    return {"tokens": tokens, "weights": weights, "push_scale": push_scale, "cotangent": cotangent, "step_count": step_count}


learning_rate = 0.5

def silu_slope(hidden):
    sigma = jax.nn.sigmoid(hidden)
    return sigma * (1.0 + hidden * (1.0 - sigma))

def reference(tokens, weights, push_scale, cotangent, step_count):
    inverse = 1.0 / math.sqrt(D)

    def one_replica(replica):
        group_weights = lax.dynamic_slice_in_dim(weights, 4 * replica, 4, 0).astype(jnp.float32)
        group_scale = lax.dynamic_slice_in_dim(push_scale, 4 * replica, 4, 0).astype(jnp.float32)
        block_scale = jnp.repeat(group_scale, D // N_TP, axis=1)[:, :, None]
        scaled = (group_weights / block_scale).astype(jnp.bfloat16)
        whole_scaled = jnp.concatenate([scaled[0], scaled[1], scaled[2], scaled[3]], axis=1)
        token_rows = lax.dynamic_slice_in_dim(tokens, replica * TOK_GROUP, TOK_GROUP, 0)
        hidden = jnp.dot(token_rows, whole_scaled, preferred_element_type=jnp.float32) * inverse
        group_cot = lax.dynamic_slice_in_dim(cotangent, 4 * replica, 4, 0)
        cot_rows = jnp.concatenate([group_cot[0], group_cot[1], group_cot[2], group_cot[3]], axis=0).T
        slope_grad = (cot_rows.astype(jnp.float32) * silu_slope(hidden)).astype(jnp.bfloat16)
        weight_grad = jnp.dot(token_rows.T, slope_grad, preferred_element_type=jnp.float32) * inverse
        full_weights = jnp.concatenate([group_weights[0], group_weights[1], group_weights[2], group_weights[3]], axis=1)
        stepped = (full_weights - learning_rate * weight_grad).astype(jnp.bfloat16)
        return jnp.stack([stepped[:, number * QUARTER_FF:(number + 1) * QUARTER_FF] for number in range(4)])
    stepped = lax.map(one_replica, jnp.arange(REPLICAS, dtype=jnp.int32)).reshape(N_REP, D, QUARTER_FF)
    levels = REPLICAS.bit_length() - 1
    distance = jnp.left_shift(jnp.int32(4), (step_count[0] % levels).astype(jnp.int32))
    source = jnp.roll(stepped, distance, axis=0)
    mixed_weights = (0.5 * (stepped.astype(jnp.float32) + source.astype(jnp.float32))).astype(jnp.bfloat16)
    scales = push_scale.astype(jnp.float32)
    mixed_scale = 0.5 * (scales + jnp.roll(scales, distance, axis=0))
    return (mixed_weights, mixed_scale)
```

```python
import functools
import math

import jax
import jax.numpy as jnp
from jax import lax
from jax.experimental import pallas as pl
from jax.experimental.pallas import tpu as pltpu
from jax.sharding import PartitionSpec as P

learning_rate = 0.5
MESH = pl.DeviceIdType.MESH
CHUNKS = (48, 96, 144, 144)
STARTS = tuple(sum(CHUNKS[:i]) for i in range(len(CHUNKS)))
RELAYED = ((3,), (3,), (2, 3), ())
LANES = 128


def moved(rep, dz, dy):
    z, y, x = rep // 16, rep // 2 % 8, rep % 2
    return (z + dz + 8) % 8 * 16 + (y + dy + 8) % 8 * 2 + x


def kernel(
    level,
    inverse,
    tok_hbm,
    w_hbm,
    scale_ref,
    cot_hbm,
    out_hbm,
    mixed_scale_ref,
    w,
    xt,
    tok,
    cot,
    part,
    part_rx,
    slope,
    rx,
    relay,
    out,
    sc_own,
    sc_rx,
    load_sem,
    tok_s,
    tok_r,
    rs_s,
    rs_r,
    ag_s,
    ag_r,
    mx_s,
    mx_r,
    rl_r,
    fw_s,
    sc_sem,
    out_sem,
):
    rep, tp = lax.axis_index("rep"), lax.axis_index("tp")
    n_rep, n_tp = lax.axis_size("rep"), lax.axis_size("tp")
    rows, width = tok_hbm.shape
    hidden_units = w_hbm.shape[1]
    share = hidden_units // n_tp
    count = len(CHUNKS)
    shift = 4 * 2**level
    relayed = RELAYED if level in (0, 3) else ((),) * count
    back = (0, 3) if level == 0 else (3, 0)

    member = rep % 4
    flip1 = 1 - 2 * (member % 2)
    flip2 = 2 - 4 * (member // 2)
    mates = [rep + flip1, rep + flip2, rep + flip1 + flip2]
    target = (rep + shift) % n_rep
    origin = (rep + n_rep - shift) % n_rep
    via = moved(rep, -back[0], -back[1])
    from_via = moved(rep, back[0], back[1])
    via_target = (from_via + shift) % n_rep
    last_via = moved(origin, -back[0], -back[1])

    loads = [
        pltpu.make_async_copy(w_hbm, w, load_sem.at[0]),
        pltpu.make_async_copy(
            tok_hbm, tok.at[pl.ds(pl.multiple_of(member * rows, rows), rows)], load_sem.at[1]
        ),
        pltpu.make_async_copy(cot_hbm, cot, load_sem.at[2]),
    ]
    for load in loads:
        load.start()

    senders = [(m, tp) for m in mates]
    senders += [(rep, (tp + n_tp - q) % n_tp) for q in (1, 2, 3)]
    senders += [(origin, tp)]
    if any(relayed):
        senders += [(from_via, tp), (last_via, tp)]
    barrier = pltpu.get_barrier_semaphore()
    for sender in senders:
        pl.semaphore_signal(barrier, inc=1, device_id=sender, device_id_type=MESH)
    scale = scale_ref[...].astype(jnp.float32)
    sc_own[...] = jnp.broadcast_to(scale, sc_own.shape)
    pl.semaphore_wait(barrier, len(senders))

    def send(src, dst, s, r, to):
        return pltpu.make_async_remote_copy(
            src_ref=src, dst_ref=dst, send_sem=s, recv_sem=r, device_id=to, device_id_type=MESH
        )

    own_rows = pl.ds(pl.multiple_of(member * rows, rows), rows)
    tok_copies = [
        send(tok_hbm, tok.at[own_rows], tok_s.at[i], tok_r.at[i], (m, tp))
        for i, m in enumerate(mates)
    ]
    for copy in tok_copies:
        copy.start()
    sc_copy = send(sc_own, sc_rx, sc_sem.at[0], sc_sem.at[1], (target, tp))
    sc_copy.start()

    full = hidden_units // LANES
    with jax.named_scope("transpose_in"):
        loads[0].wait()

        def turn(i, _):
            at = pl.ds(pl.multiple_of(i * LANES, LANES), LANES)
            xt[at, :] = w[:, at].T
            return 0

        lax.fori_loop(0, full, turn, 0)
        if hidden_units % LANES:
            xt[full * LANES :, :] = w[:, full * LANES :].T

    with jax.named_scope("wait_tokens"):
        loads[1].wait()
        for copy in tok_copies:
            copy.wait_recv()

    factor = inverse / scale

    def piece(owner, k):
        return pl.ds(pl.multiple_of(owner * share + STARTS[k], 16), CHUNKS[k])

    def rs_copy(k, q):
        to = (tp + q) % n_tp
        return send(
            part.at[piece(to, k)],
            part_rx.at[q - 1, pl.ds(STARTS[k], CHUNKS[k])],
            rs_s.at[k, q - 1],
            rs_r.at[k, q - 1],
            (rep, to),
        )

    def ag_copy(k, q, owner):
        return send(
            slope.at[piece(owner, k)],
            slope.at[piece(owner, k)],
            ag_s.at[k, q - 1],
            ag_r.at[k, q - 1],
            (rep, (tp + q) % n_tp),
        )

    def mix_copy(k, u):
        at = piece(u, k)
        if u in relayed[k]:
            return send(xt.at[at], relay.at[at], mx_s.at[k, u], rl_r.at[k, u], (via, tp))
        return send(xt.at[at], rx.at[at], mx_s.at[k, u], mx_r.at[k, u], (target, tp))

    def forward_copy(k, u):
        at = piece(u, k)
        return send(relay.at[at], rx.at[at], fw_s.at[k, u], mx_r.at[k, u], (via_target, tp))

    def products(k):
        with jax.named_scope("products"):

            def one(u, _):
                at = piece(u, k)
                p = lax.dot_general(
                    xt[at, :], tok[...], (((1,), (1,)), ((), ())), preferred_element_type=jnp.float32
                )
                part[at, :] = (p * factor).astype(jnp.bfloat16)
                return 0

            lax.fori_loop(0, n_tp, one, 0)

    def scatter(k):
        for q in (2, 1, 3):
            rs_copy(k, q).start()

    def slopes(k):
        with jax.named_scope("slopes"):
            for q in (1, 2, 3):
                rs_copy(k, q).wait_recv()
            mine = piece(tp, k)
            local = pl.ds(STARTS[k], CHUNKS[k])
            h = part[mine, :].astype(jnp.float32)
            for q in range(3):
                h += part_rx[q, local, :].astype(jnp.float32)
            sigma = jax.nn.sigmoid(h)
            d = sigma * (1.0 + h * (1.0 - sigma))
            slope[mine, :] = (cot[local, :].astype(jnp.float32) * d).astype(jnp.bfloat16)
            for q in (2, 1, 3):
                ag_copy(k, q, tp).start()

    def step(k):
        with jax.named_scope("step"):
            for q in (1, 2, 3):
                ag_copy(k, q, (tp + n_tp - q) % n_tp).wait_recv()
            for u in range(n_tp):
                at = piece(u, k)
                g = jnp.dot(slope[at, :], tok[...], preferred_element_type=jnp.float32)
                x = xt[at, :].astype(jnp.float32)
                xt[at, :] = (x - (learning_rate * inverse) * g).astype(jnp.bfloat16)
                mix_copy(k, u).start()

    def forward(k):
        for u in relayed[k]:
            with jax.named_scope("forward"):
                send(
                    relay.at[piece(u, k)], relay.at[piece(u, k)], fw_s.at[k, u], rl_r.at[k, u], (via, tp)
                ).wait_recv()
                forward_copy(k, u).start()

    products(0)
    scatter(0)
    products(1)
    loads[2].wait()
    slopes(0)
    scatter(1)
    for k in range(count):
        step(k)
        if k + 2 < count:
            products(k + 2)
        if k + 1 < count:
            slopes(k + 1)
        if k + 2 < count:
            scatter(k + 2)
        if k >= 1:
            forward(k - 1)
    forward(count - 1)

    blocks = [(i, min(i + LANES, hidden_units)) for i in range(0, hidden_units, LANES)]
    arrived = set()
    done = set()
    sc_copy.wait()
    mixed_scale_ref[...] = (0.5 * (sc_own[...] + sc_rx[...]))[:1, :1]
    for k in range(count):
        for u in range(n_tp):
            with jax.named_scope("wait_mix"):
                send(
                    rx.at[piece(u, k)], rx.at[piece(u, k)], mx_s.at[k, u], mx_r.at[k, u], (target, tp)
                ).wait_recv()
            begin = u * share + STARTS[k]
            arrived.update(range(begin, begin + CHUNKS[k], 16))
            for a, b in blocks:
                if a not in done and arrived.issuperset(range(a, b, 16)):
                    done.add(a)
                    with jax.named_scope("mix"):
                        m = 0.5 * (xt[a:b, :].astype(jnp.float32) + rx[a:b, :].astype(jnp.float32))
                        out[:, a:b] = m.astype(jnp.bfloat16).T
    store = pltpu.make_async_copy(out, out_hbm, out_sem)
    store.start()

    for copy in tok_copies:
        copy.wait_send()
    loads_left = []
    for k in range(count):
        for q in (1, 2, 3):
            rs_copy(k, q).wait_send()
            ag_copy(k, q, tp).wait_send()
        for u in range(n_tp):
            mix_copy(k, u).wait_send()
        for u in relayed[k]:
            forward_copy(k, u).wait_send()
    store.wait()


def one_level(level, inverse, tokens, weights, push_scale, cotangent):
    rows, width = tokens.shape
    hidden_units = weights.shape[1]
    share, all_tokens = cotangent.shape
    count = len(CHUNKS)
    half, single = jnp.bfloat16, jnp.float32
    dma = pltpu.SemaphoreType.DMA
    anywhere, vmem = pl.BlockSpec(memory_space=pl.ANY), pl.BlockSpec(memory_space=pltpu.VMEM)
    return pl.pallas_call(
        functools.partial(kernel, level, inverse),
        out_shape=(
            jax.ShapeDtypeStruct((width, hidden_units), half),
            jax.ShapeDtypeStruct((1, 1), single),
        ),
        in_specs=[anywhere, anywhere, vmem, anywhere],
        out_specs=(anywhere, vmem),
        scratch_shapes=[
            pltpu.VMEM((width, hidden_units), half),
            pltpu.VMEM((hidden_units, width), half),
            pltpu.VMEM((all_tokens, width), half),
            pltpu.VMEM((share, all_tokens), half),
            pltpu.VMEM((hidden_units, all_tokens), half),
            pltpu.VMEM((3, share, all_tokens), half),
            pltpu.VMEM((hidden_units, all_tokens), half),
            pltpu.VMEM((hidden_units, width), half),
            pltpu.VMEM((hidden_units, width), half),
            pltpu.VMEM((width, hidden_units), half),
            pltpu.VMEM((8, LANES), single),
            pltpu.VMEM((8, LANES), single),
            dma((3,)),
            dma((3,)),
            dma((3,)),
            dma((count, 3)),
            dma((count, 3)),
            dma((count, 3)),
            dma((count, 3)),
            dma((count, 4)),
            dma((count, 4)),
            dma((count, 4)),
            dma((count, 4)),
            dma((2,)),
            dma,
        ],
        compiler_params=pltpu.CompilerParams(
            collective_id=level, has_side_effects=True, vmem_limit_bytes=48 * 2**20
        ),
        cost_estimate=pl.CostEstimate(
            flops=4 * width * hidden_units * all_tokens,
            bytes_accessed=8 * width * hidden_units,
            transcendentals=share * all_tokens,
        ),
        name="push_step",
    )(tokens, weights, push_scale, cotangent)


def per_device(tokens, weights, push_scale, cotangent, step_count):
    inverse = 1.0 / math.sqrt(tokens.shape[1] * lax.axis_size("tp"))
    levels = lax.axis_size("rep").bit_length() - 3
    mixed, mixed_scale = lax.switch(
        step_count[0] % levels,
        [functools.partial(one_level, level, inverse) for level in range(levels)],
        tokens,
        weights[0],
        push_scale,
        cotangent[0],
    )
    return mixed[None], mixed_scale


def solution(mesh):
    placed = (P("rep", "tp"), P("rep", "tp", None), P("rep", "tp"), P("rep", "tp", None), P())
    return jax.shard_map(
        per_device,
        mesh=mesh,
        in_specs=placed,
        out_specs=(P("rep", "tp", None), P("rep", "tp")),
        check_vma=False,
    )
```

```python
import functools
import math

import jax
import jax.numpy as jnp
from jax import lax
from jax.experimental import pallas as pl
from jax.experimental.pallas import tpu as pltpu
from jax.sharding import PartitionSpec as P

learning_rate = 0.5
MESH = pl.DeviceIdType.MESH
CHUNKS = (32, 64, 96, 112, 128)
STRAIGHT = (True, False, False, False, False)
RELAYED = ((3,), (3,), (3,), (2, 3), ())
LANES = 128
VMEM_BYTES = 40 * 2**20
FULL = 9


def moved(rep, dz, dy):
    z, y, x = rep // 16, rep // 2 % 8, rep % 2
    return (z + dz + 8) % 8 * 16 + (y + dy + 8) % 8 * 2 + x


def kernel(
    level,
    inverse,
    stage,
    tok_hbm,
    w_hbm,
    scale_ref,
    cot_hbm,
    out_hbm,
    mixed_scale_ref,
    xt,
    tok,
    cot,
    part,
    part_rx,
    part_sum,
    slope,
    rx,
    relay,
    sc_own,
    sc_rx,
    load_sem,
    tok_s,
    tok_r,
    rs_s,
    rs_r,
    ag_s,
    ag_r,
    mx_s,
    mx_r,
    rl_r,
    fw_s,
    sc_sem,
    out_sem,
):
    rep, tp = lax.axis_index("rep"), lax.axis_index("tp")
    n_rep, n_tp = lax.axis_size("rep"), lax.axis_size("tp")
    rows = tok_hbm.shape[0]
    share = w_hbm.shape[0] // n_tp
    count = len(CHUNKS)
    starts = [sum(CHUNKS[:k]) for k in range(count)]
    shift = 4 * 2**level
    relayed = RELAYED if level in (0, 3) else ((),) * count
    back = (0, 3) if level == 0 else (3, 0)

    member = rep % 4
    flip1 = 1 - 2 * (member % 2)
    flip2 = 2 - 4 * (member // 2)
    mates = [rep + flip1, rep + flip2, rep + flip1 + flip2]
    core_mate = tp + 1 - 2 * (tp % 2)
    x_mate = (tp + 2) % n_tp
    other = (core_mate + 2) % n_tp
    peers = [core_mate, x_mate, other]
    target = (rep + shift) % n_rep
    origin = (rep + n_rep - shift) % n_rep
    via = moved(rep, -back[0], -back[1])
    from_via = moved(rep, back[0], back[1])
    via_target = (from_via + shift) % n_rep
    last_via = moved(origin, -back[0], -back[1])

    own_rows = pl.ds(pl.multiple_of(member * rows, rows), rows)
    loads = [
        pltpu.make_async_copy(tok_hbm, tok.at[own_rows], load_sem.at[0]),
        pltpu.make_async_copy(w_hbm, xt, load_sem.at[1]),
        pltpu.make_async_copy(cot_hbm, cot, load_sem.at[2]),
    ]
    for load in loads:
        load.start()

    senders = [(m, tp) for m in mates] + [(rep, p) for p in peers] + [(origin, tp)]
    if any(relayed):
        senders += [(from_via, tp), (last_via, tp)]
    barrier = pltpu.get_barrier_semaphore()
    for sender in senders:
        pl.semaphore_signal(barrier, inc=1, device_id=sender, device_id_type=MESH)
    scale = scale_ref[...].astype(jnp.float32)
    sc_own[...] = jnp.broadcast_to(scale, sc_own.shape)
    pl.semaphore_wait(barrier, len(senders))

    def send(src, dst, s, r, to):
        return pltpu.make_async_remote_copy(
            src_ref=src, dst_ref=dst, send_sem=s, recv_sem=r, device_id=to, device_id_type=MESH
        )

    tok_copies = [
        send(tok_hbm, tok.at[own_rows], tok_s.at[i], tok_r.at[i], (m, tp))
        for i, m in enumerate(mates)
    ]
    for i in (2, 0, 1):
        tok_copies[i].start()
    sc_copy = send(sc_own, sc_rx, sc_sem.at[0], sc_sem.at[1], (target, tp))
    sc_copy.start()
    for load in loads:
        load.wait()
    for copy in tok_copies:
        copy.wait_recv()

    factor = inverse / scale

    def local(k):
        return pl.ds(starts[k], CHUNKS[k])

    def piece(owner, k):
        return pl.ds(pl.multiple_of(owner * share + starts[k], 16), CHUNKS[k])

    def rs_copy(k, q):
        if STRAIGHT[k]:
            src, to = part.at[piece(peers[q], k)], peers[q]
        elif q == 0:
            src, to = part.at[piece(core_mate, k)], core_mate
        elif q == 1:
            src, to = part.at[piece(other, k)], core_mate
        else:
            src, to = part_sum.at[local(k)], x_mate
        return send(src, part_rx.at[q, local(k)], rs_s.at[k, q], rs_r.at[k, q], (rep, to))

    def ag_copy(k, q):
        if STRAIGHT[k] or q < 2:
            owner, to = tp, peers[q]
        else:
            owner, to = x_mate, core_mate
        at = slope.at[piece(owner, k)]
        return send(at, at, ag_s.at[k, q], ag_r.at[k, q], (rep, to))

    def ag_wait(k, q):
        at = slope.at[piece(peers[q], k)]
        send(at, at, ag_s.at[k, q], ag_r.at[k, q], (rep, peers[q])).wait_recv()

    def mix_copy(k, u):
        at = piece(u, k)
        if u in relayed[k]:
            return send(xt.at[at], relay.at[at], mx_s.at[k, u], rl_r.at[k, u], (via, tp))
        return send(xt.at[at], rx.at[at], mx_s.at[k, u], mx_r.at[k, u], (target, tp))

    def forward_copy(k, u):
        at = piece(u, k)
        return send(relay.at[at], rx.at[at], fw_s.at[k, u], mx_r.at[k, u], (via_target, tp))

    def products(k):
        def one(u, _):
            at = piece(u, k)
            p = lax.dot_general(
                xt[at, :], tok[...], (((1,), (1,)), ((), ())), preferred_element_type=jnp.float32
            )
            part[at, :] = (p * factor).astype(jnp.bfloat16)
            return 0

        lax.fori_loop(0, n_tp, one, 0)

    def scatter(k):
        for q in (1, 2, 0) if STRAIGHT[k] else (1, 0):
            rs_copy(k, q).start()

    def scatter_on(k):
        if not STRAIGHT[k]:
            rs_copy(k, 1).wait_recv()
            total = part[piece(x_mate, k), :].astype(jnp.float32)
            total += part_rx[1, local(k), :].astype(jnp.float32)
            part_sum[local(k), :] = total.astype(jnp.bfloat16)
            rs_copy(k, 2).start()

    def slopes(k):
        mine = piece(tp, k)
        slots = (0, 1, 2) if STRAIGHT[k] else (0, 2)
        h = part[mine, :].astype(jnp.float32)
        for q in slots:
            rs_copy(k, q).wait_recv()
        for q in slots:
            h += part_rx[q, local(k), :].astype(jnp.float32)
        sigma = jax.nn.sigmoid(h)
        d = sigma * (1.0 + h * (1.0 - sigma))
        slope[mine, :] = (cot[local(k), :].astype(jnp.float32) * d).astype(jnp.bfloat16)
        for q in (1, 2, 0) if STRAIGHT[k] else (1, 0):
            ag_copy(k, q).start()

    def step(k):
        ag_wait(k, 1)
        if not STRAIGHT[k]:
            ag_copy(k, 2).start()
        ag_wait(k, 0)
        ag_wait(k, 2)
        for u in range(n_tp):
            at = piece(u, k)
            g = jnp.dot(slope[at, :], tok[...], preferred_element_type=jnp.float32)
            x = xt[at, :].astype(jnp.float32)
            xt[at, :] = (x - (learning_rate * inverse) * g).astype(jnp.bfloat16)
            if stage > 2:
                mix_copy(k, u).start()

    def forward(k):
        for u in relayed[k]:
            at = relay.at[piece(u, k)]
            send(at, at, fw_s.at[k, u], rl_r.at[k, u], (via, tp)).wait_recv()
            forward_copy(k, u).start()

    if stage > 1:
        products(0)
        scatter(0)
        products(1)
        scatter_on(0)
        for k in range(count):
            slopes(k)
            if k + 1 < count:
                scatter(k + 1)
                if k + 2 < count:
                    products(k + 2)
                scatter_on(k + 1)
            step(k)
            if k >= 1 and stage > 2:
                forward(k - 1)
    if stage > 2:
        forward(count - 1)

    stores = []
    sc_copy.wait()
    mixed_scale_ref[...] = (0.5 * (sc_own[...] + sc_rx[...]))[:1, :1]
    for k in range(count):
        for u in range(n_tp):
            at = piece(u, k)
            if stage > 2:
                send(rx.at[at], rx.at[at], mx_s.at[k, u], mx_r.at[k, u], (target, tp)).wait_recv()
            m = 0.5 * (xt[at, :].astype(jnp.float32) + rx[at, :].astype(jnp.float32))
            rx[at, :] = m.astype(jnp.bfloat16)
            store = pltpu.make_async_copy(rx.at[at], out_hbm.at[at], out_sem.at[k, u])
            store.start()
            stores.append(store)

    for copy in tok_copies:
        copy.wait_send()
    for k in range(count):
        for q in range(3):
            if stage > 1:
                rs_copy(k, q).wait_send()
                ag_copy(k, q).wait_send()
        if stage > 2:
            for u in range(n_tp):
                mix_copy(k, u).wait_send()
            for u in relayed[k]:
                forward_copy(k, u).wait_send()
    for store in stores:
        store.wait()


def one_level(level, inverse, stage, tokens, weights, push_scale, cotangent):
    hidden_units, width = weights.shape
    share, all_tokens = cotangent.shape
    count = len(CHUNKS)
    half, single = jnp.bfloat16, jnp.float32
    dma = pltpu.SemaphoreType.DMA
    anywhere, vmem = pl.BlockSpec(memory_space=pl.ANY), pl.BlockSpec(memory_space=pltpu.VMEM)
    return pl.pallas_call(
        functools.partial(kernel, level, inverse, stage),
        out_shape=(
            jax.ShapeDtypeStruct((hidden_units, width), half),
            jax.ShapeDtypeStruct((1, 1), single),
        ),
        in_specs=[anywhere, anywhere, vmem, anywhere],
        out_specs=(anywhere, vmem),
        scratch_shapes=[
            pltpu.VMEM((hidden_units, width), half),
            pltpu.VMEM((all_tokens, width), half),
            pltpu.VMEM((share, all_tokens), half),
            pltpu.VMEM((hidden_units, all_tokens), half),
            pltpu.VMEM((3, share, all_tokens), half),
            pltpu.VMEM((share, all_tokens), half),
            pltpu.VMEM((hidden_units, all_tokens), half),
            pltpu.VMEM((hidden_units, width), half),
            pltpu.VMEM((hidden_units, width), half),
            pltpu.VMEM((8, LANES), single),
            pltpu.VMEM((8, LANES), single),
            dma((3,)),
            dma((3,)),
            dma((3,)),
            dma((count, 3)),
            dma((count, 3)),
            dma((count, 3)),
            dma((count, 3)),
            dma((count, 4)),
            dma((count, 4)),
            dma((count, 4)),
            dma((count, 4)),
            dma((2,)),
            dma((count, 4)),
        ],
        compiler_params=pltpu.CompilerParams(
            collective_id=level, has_side_effects=True, vmem_limit_bytes=VMEM_BYTES
        ),
        cost_estimate=pl.CostEstimate(
            flops=4 * width * hidden_units * all_tokens,
            bytes_accessed=4 * width * hidden_units,
            transcendentals=share * all_tokens,
        ),
        name="push_step",
    )(tokens, weights, push_scale, cotangent)


def per_device(tokens, weights, push_scale, cotangent, step_count):
    inverse = 1.0 / math.sqrt(tokens.shape[1] * lax.axis_size("tp"))
    levels = lax.axis_size("rep").bit_length() - 3
    mixed, mixed_scale = lax.switch(
        step_count[0] % levels,
        [functools.partial(one_level, level, inverse, FULL) for level in range(levels)],
        tokens,
        weights[0].T,
        push_scale,
        cotangent[0],
    )
    return mixed.T[None], mixed_scale


def solution(mesh):
    placed = (P("rep", "tp"), P("rep", "tp", None), P("rep", "tp"), P("rep", "tp", None), P())
    return jax.shard_map(
        per_device,
        mesh=mesh,
        in_specs=placed,
        out_specs=(P("rep", "tp", None), P("rep", "tp")),
        check_vma=False,
    )
```

```python
import functools
import math

import jax
import jax.numpy as jnp
from jax import lax
from jax.experimental import pallas as pl
from jax.experimental.pallas import tpu as pltpu
from jax.sharding import PartitionSpec as P

learning_rate = 0.5
MESH = pl.DeviceIdType.MESH
CHUNKS = (48, 80, 96, 112, 96)
CHUNKS_RELAYED = (32, 64, 96, 112, 128)
STRAIGHT = (True, False, False, False, False)
RELAYED = ((3,), (3,), (3,), (2, 3), ())
LANES = 128
VMEM_BYTES = 40 * 2**20


def moved(rep, dz, dy):
    z, y, x = rep // 16, rep // 2 % 8, rep % 2
    return (z + dz + 8) % 8 * 16 + (y + dy + 8) % 8 * 2 + x


def chunks_of(level):
    return CHUNKS_RELAYED if level in (0, 3) else CHUNKS


def kernel(
    level,
    inverse,
    tok_hbm,
    w_hbm,
    scale_ref,
    cot_hbm,
    out_hbm,
    mixed_scale_ref,
    xt,
    tok,
    cot,
    part,
    part_rx,
    part_sum,
    slope,
    rx,
    relay,
    sc_own,
    sc_rx,
    load_sem,
    tok_s,
    tok_r,
    rs_s,
    rs_r,
    ag_s,
    ag_r,
    mx_s,
    mx_r,
    rl_r,
    fw_s,
    sc_sem,
    out_sem,
):
    rep, tp = lax.axis_index("rep"), lax.axis_index("tp")
    n_rep, n_tp = lax.axis_size("rep"), lax.axis_size("tp")
    rows = tok_hbm.shape[0]
    share = w_hbm.shape[0] // n_tp
    chunks = chunks_of(level)
    count = len(chunks)
    starts = [sum(chunks[:k]) for k in range(count)]
    shift = 4 * 2**level
    relayed = RELAYED if level in (0, 3) else ((),) * count
    back = (0, 3) if level == 0 else (3, 0)

    member = rep % 4
    flip1 = 1 - 2 * (member % 2)
    flip2 = 2 - 4 * (member // 2)
    mates = [rep + flip1, rep + flip2, rep + flip1 + flip2]
    core_mate = tp + 1 - 2 * (tp % 2)
    x_mate = (tp + 2) % n_tp
    other = (core_mate + 2) % n_tp
    peers = [core_mate, x_mate, other]
    target = (rep + shift) % n_rep
    origin = (rep + n_rep - shift) % n_rep
    via = moved(rep, -back[0], -back[1])
    from_via = moved(rep, back[0], back[1])
    via_target = (from_via + shift) % n_rep
    last_via = moved(origin, -back[0], -back[1])

    own_rows = pl.ds(pl.multiple_of(member * rows, rows), rows)
    loads = [
        pltpu.make_async_copy(tok_hbm, tok.at[own_rows], load_sem.at[0]),
        pltpu.make_async_copy(w_hbm, xt, load_sem.at[1]),
        pltpu.make_async_copy(cot_hbm, cot, load_sem.at[2]),
    ]
    for load in loads:
        load.start()

    senders = [(m, tp) for m in mates] + [(rep, p) for p in peers] + [(origin, tp)]
    if any(relayed):
        senders += [(from_via, tp), (last_via, tp)]
    barrier = pltpu.get_barrier_semaphore()
    for sender in senders:
        pl.semaphore_signal(barrier, inc=1, device_id=sender, device_id_type=MESH)
    scale = scale_ref[...].astype(jnp.float32)
    sc_own[...] = jnp.broadcast_to(scale, sc_own.shape)
    pl.semaphore_wait(barrier, len(senders))

    def send(src, dst, s, r, to):
        return pltpu.make_async_remote_copy(
            src_ref=src, dst_ref=dst, send_sem=s, recv_sem=r, device_id=to, device_id_type=MESH
        )

    tok_copies = [
        send(tok_hbm, tok.at[own_rows], tok_s.at[i], tok_r.at[i], (m, tp))
        for i, m in enumerate(mates)
    ]
    for i in (2, 0, 1):
        tok_copies[i].start()
    sc_copy = send(sc_own, sc_rx, sc_sem.at[0], sc_sem.at[1], (target, tp))
    sc_copy.start()
    for load in loads:
        load.wait()
    for copy in tok_copies:
        copy.wait_recv()

    factor = inverse / scale

    def local(k):
        return pl.ds(starts[k], chunks[k])

    def piece(owner, k):
        return pl.ds(pl.multiple_of(owner * share + starts[k], 16), chunks[k])

    def rs_copy(k, q):
        if STRAIGHT[k]:
            src, to = part.at[piece(peers[q], k)], peers[q]
        elif q == 0:
            src, to = part.at[piece(core_mate, k)], core_mate
        elif q == 1:
            src, to = part.at[piece(other, k)], core_mate
        else:
            src, to = part_sum.at[local(k)], x_mate
        return send(src, part_rx.at[q, local(k)], rs_s.at[k, q], rs_r.at[k, q], (rep, to))

    def ag_copy(k, q):
        if STRAIGHT[k] or q < 2:
            owner, to = tp, peers[q]
        else:
            owner, to = x_mate, core_mate
        at = slope.at[piece(owner, k)]
        return send(at, at, ag_s.at[k, q], ag_r.at[k, q], (rep, to))

    def ag_wait(k, q):
        at = slope.at[piece(peers[q], k)]
        send(at, at, ag_s.at[k, q], ag_r.at[k, q], (rep, peers[q])).wait_recv()

    def mix_copy(k, u):
        at = piece(u, k)
        if u in relayed[k]:
            return send(xt.at[at], relay.at[at], mx_s.at[k, u], rl_r.at[k, u], (via, tp))
        return send(xt.at[at], rx.at[at], mx_s.at[k, u], mx_r.at[k, u], (target, tp))

    def forward_copy(k, u):
        at = piece(u, k)
        return send(relay.at[at], rx.at[at], fw_s.at[k, u], mx_r.at[k, u], (via_target, tp))

    def products(k):
        def one(u, _):
            at = piece(u, k)
            p = lax.dot_general(
                xt[at, :], tok[...], (((1,), (1,)), ((), ())), preferred_element_type=jnp.float32
            )
            part[at, :] = (p * factor).astype(jnp.bfloat16)
            return 0

        lax.fori_loop(0, n_tp, one, 0)

    def scatter(k):
        for q in (1, 2, 0) if STRAIGHT[k] else (1, 0):
            rs_copy(k, q).start()

    def scatter_on(k):
        if not STRAIGHT[k]:
            rs_copy(k, 1).wait_recv()
            total = part[piece(x_mate, k), :].astype(jnp.float32)
            total += part_rx[1, local(k), :].astype(jnp.float32)
            part_sum[local(k), :] = total.astype(jnp.bfloat16)
            rs_copy(k, 2).start()

    def slopes(k):
        mine = piece(tp, k)
        slots = (0, 1, 2) if STRAIGHT[k] else (0, 2)
        h = part[mine, :].astype(jnp.float32)
        for q in slots:
            rs_copy(k, q).wait_recv()
        for q in slots:
            h += part_rx[q, local(k), :].astype(jnp.float32)
        sigma = jax.nn.sigmoid(h)
        d = sigma * (1.0 + h * (1.0 - sigma))
        slope[mine, :] = (cot[local(k), :].astype(jnp.float32) * d).astype(jnp.bfloat16)
        for q in (1, 2, 0) if STRAIGHT[k] else (1, 0):
            ag_copy(k, q).start()

    def step(k):
        ag_wait(k, 1)
        if not STRAIGHT[k]:
            ag_copy(k, 2).start()
        ag_wait(k, 0)
        ag_wait(k, 2)
        for u in range(n_tp):
            at = piece(u, k)
            g = jnp.dot(slope[at, :], tok[...], preferred_element_type=jnp.float32)
            x = xt[at, :].astype(jnp.float32)
            xt[at, :] = (x - (learning_rate * inverse) * g).astype(jnp.bfloat16)
            mix_copy(k, u).start()

    def forward(k):
        for u in relayed[k]:
            at = relay.at[piece(u, k)]
            send(at, at, fw_s.at[k, u], rl_r.at[k, u], (via, tp)).wait_recv()
            forward_copy(k, u).start()

    products(0)
    scatter(0)
    products(1)
    if any(relayed):
        scatter_on(0)
        for k in range(count):
            slopes(k)
            if k + 1 < count:
                scatter(k + 1)
                if k + 2 < count:
                    products(k + 2)
                scatter_on(k + 1)
            step(k)
            if k >= 1:
                forward(k - 1)
        forward(count - 1)
    else:
        scatter(1)
        scatter_on(0)
        scatter_on(1)
        products(2)
        scatter(2)
        slopes(0)
        for k in range(count):
            if k + 1 < count:
                slopes(k + 1)
            if k + 2 < count:
                scatter_on(k + 2)
            step(k)
            if k + 3 < count:
                products(k + 3)
                scatter(k + 3)

    stores = []
    sc_copy.wait()
    mixed_scale_ref[...] = (0.5 * (sc_own[...] + sc_rx[...]))[:1, :1]
    for k in range(count):
        for u in range(n_tp):
            at = piece(u, k)
            send(rx.at[at], rx.at[at], mx_s.at[k, u], mx_r.at[k, u], (target, tp)).wait_recv()
            m = 0.5 * (xt[at, :].astype(jnp.float32) + rx[at, :].astype(jnp.float32))
            rx[at, :] = m.astype(jnp.bfloat16)
            store = pltpu.make_async_copy(rx.at[at], out_hbm.at[at], out_sem.at[k, u])
            store.start()
            stores.append(store)

    for copy in tok_copies:
        copy.wait_send()
    for k in range(count):
        for q in range(3):
            rs_copy(k, q).wait_send()
            ag_copy(k, q).wait_send()
        for u in range(n_tp):
            mix_copy(k, u).wait_send()
        for u in relayed[k]:
            forward_copy(k, u).wait_send()
    for store in stores:
        store.wait()


def one_level(level, inverse, tokens, weights, push_scale, cotangent):
    hidden_units, width = weights.shape
    share, all_tokens = cotangent.shape
    count = len(chunks_of(level))
    half, single = jnp.bfloat16, jnp.float32
    dma = pltpu.SemaphoreType.DMA
    anywhere, vmem = pl.BlockSpec(memory_space=pl.ANY), pl.BlockSpec(memory_space=pltpu.VMEM)
    return pl.pallas_call(
        functools.partial(kernel, level, inverse),
        out_shape=(
            jax.ShapeDtypeStruct((hidden_units, width), half),
            jax.ShapeDtypeStruct((1, 1), single),
        ),
        in_specs=[anywhere, anywhere, vmem, anywhere],
        out_specs=(anywhere, vmem),
        scratch_shapes=[
            pltpu.VMEM((hidden_units, width), half),
            pltpu.VMEM((all_tokens, width), half),
            pltpu.VMEM((share, all_tokens), half),
            pltpu.VMEM((hidden_units, all_tokens), half),
            pltpu.VMEM((3, share, all_tokens), half),
            pltpu.VMEM((share, all_tokens), half),
            pltpu.VMEM((hidden_units, all_tokens), half),
            pltpu.VMEM((hidden_units, width), half),
            pltpu.VMEM((hidden_units, width), half),
            pltpu.VMEM((8, LANES), single),
            pltpu.VMEM((8, LANES), single),
            dma((3,)),
            dma((3,)),
            dma((3,)),
            dma((count, 3)),
            dma((count, 3)),
            dma((count, 3)),
            dma((count, 3)),
            dma((count, 4)),
            dma((count, 4)),
            dma((count, 4)),
            dma((count, 4)),
            dma((2,)),
            dma((count, 4)),
        ],
        compiler_params=pltpu.CompilerParams(
            collective_id=level, has_side_effects=True, vmem_limit_bytes=VMEM_BYTES
        ),
        cost_estimate=pl.CostEstimate(
            flops=4 * width * hidden_units * all_tokens,
            bytes_accessed=4 * width * hidden_units,
            transcendentals=share * all_tokens,
        ),
        name="push_step",
    )(tokens, weights, push_scale, cotangent)


def per_device(tokens, weights, push_scale, cotangent, step_count):
    inverse = 1.0 / math.sqrt(tokens.shape[1] * lax.axis_size("tp"))
    levels = lax.axis_size("rep").bit_length() - 3
    mixed, mixed_scale = lax.switch(
        step_count[0] % levels,
        [functools.partial(one_level, level, inverse) for level in range(levels)],
        tokens,
        weights[0].T,
        push_scale,
        cotangent[0],
    )
    return mixed.T[None], mixed_scale


def solution(mesh):
    placed = (P("rep", "tp"), P("rep", "tp", None), P("rep", "tp"), P("rep", "tp", None), P())
    return jax.shard_map(
        per_device,
        mesh=mesh,
        in_specs=placed,
        out_specs=(P("rep", "tp", None), P("rep", "tp")),
        check_vma=False,
    )
```
